32 devices in a mesh: band: 8 (over y, x, core), grid: 4 (over z).
Axes of the slice: x: 2, y: 2, z: 4, core: 2. Of those that a mesh axis runs over, the one named last changes fastest.
Arguments:
- orbitals: float32 [32, 48, 2304], P('band', 'grid'), may hold values from -5.5 to 6.6
- occupation: int32 [32], P('band'), may hold values from 0 to 2
- cutoff: int32 [], replicated, may hold values from 144 to 1728
Outputs:
- exchange_term: float32 [32, 48, 2304], P('band', 'grid')
The draws below stay inside these ranges and needn't reach their ends.
All inputs are finite; a program needn't handle non-finite values.
Results may differ from the reference program's by a relative error of at most 0.00005.
Values sent between devices are 32-bit elements; how exact they have to be, the bound alone decides.
A program may use at most 128 MiB of HBM per device.

```python
import jax
import jax.numpy as jnp
from jax import lax

G = 48
M = 32


def draw_orbitals(key, part):
    rough = jnp.clip(jax.random.normal(key, (M, G, G * G), jnp.float32), -5.5, 5.5)
    return rough


def set_ends(values, rng, low, largest):
    longest = values.shape.index(max(values.shape))
    spots = []
    for shift in (0, 1):
        where = [jax.random.randint(jax.random.fold_in(rng, axis), (), 0, length) for axis, length in enumerate(values.shape)]
        where[longest] = (where[longest] + shift) % values.shape[longest]
        spots.append(tuple(where))
    return values.at[spots[0]].set(low).at[spots[1]].set(largest)


def setup_inputs(seed: int = 0) -> dict:
    splits = jax.random.split(jax.random.key(seed), 4)
    orbitals = draw_orbitals(jax.random.fold_in(splits[3], 71), 0)
    occupation = set_ends(jax.random.randint(splits[1], (M,), 0, 3), jax.random.fold_in(splits[1], 1), 0, 2).astype(jnp.int32)
    cutoff = jax.random.randint(splits[2], (), G * G // 16, 3 * (G // 2) * (G // 2) + 1).astype(jnp.int32)
    return dict(orbitals=orbitals, occupation=occupation, cutoff=cutoff)


screen_alpha = 2.0
screen_scale = 4.0


def reference(orbitals, occupation, cutoff):
    fields = orbitals.reshape(M, G, G, G)
    position = jnp.arange(G, dtype=jnp.int32)
    signed = jnp.where(position <= G // 2, position, position - G)
    shells = signed[:, None, None] ** 2 + signed[None, :, None] ** 2 + signed[None, None, :] ** 2
    ratios = shells.astype(jnp.float32) / screen_alpha
    screen = jnp.where(shells > 0, (1.0 - jnp.exp(-ratios)) / jnp.maximum(ratios, 1.0 / screen_alpha), 1.0)
    kernel = jnp.where(shells <= cutoff, screen_scale * screen, 0.0).astype(jnp.float32)
    weights = occupation.astype(jnp.float32) * 0.5

    def apply_row(orbital):
        densities = orbital[None] * fields
        spectrum = jnp.fft.fftn(densities, axes=(1, 2, 3)) * kernel[None]
        potential = jnp.real(jnp.fft.ifftn(spectrum, axes=(1, 2, 3)))
        return -jnp.sum(weights[:, None, None, None] * fields * potential, axis=0)

    return lax.map(apply_row, fields).reshape(M, G, G * G).astype(jnp.float32)
```

```python
import functools

import jax
import jax.numpy as jnp
import ml_dtypes
import numpy as np
from jax import lax
from jax.experimental import pallas as pl
from jax.experimental.pallas import tpu as pltpu
from jax.sharding import PartitionSpec as P

screen_alpha = 2.0
screen_scale = 4.0


def split_halves(table):
    high = table.astype(ml_dtypes.bfloat16)
    low = (table - high.astype(np.float64)).astype(ml_dtypes.bfloat16)
    return high, low


@functools.cache
def transform_tables(extent):
    half = extent // 2
    position = np.arange(extent)
    angles = 2.0 * np.pi / extent * (position[:, None] * position[None, :] % extent)
    cas = np.cos(angles) + np.sin(angles)
    planes = [split_halves(np.kron(cas[:half, e::2], cas)) for e in (0, 1)]
    plane_tables = np.stack([np.stack(p) for p in planes])
    high, low = split_halves(cas)
    line_table = np.concatenate([high, high, low], axis=1)
    signed = np.where(position <= half, position, position - extent) ** 2
    order = np.concatenate([position[0::2], position[1::2]])
    shells = signed[:, None, None] + signed[order][None, :, None] + signed[None, None, :]
    shells = shells.reshape(extent, extent * extent).astype(np.int32)
    ratios = shells / screen_alpha
    screen = np.where(shells > 0, (1.0 - np.exp(-ratios)) / np.maximum(ratios, 0.1), 1.0)
    screen = (screen * (screen_scale / extent**3)).astype(np.float32)
    return plane_tables, line_table, shells, screen


@functools.cache
def pair_lists(bands, grids, count):
    chips = bands // 2
    parts = max(1, grids // chips)
    assert chips * parts == grids and count % parts == 0
    visitors = count // parts
    lists = []
    for g in range(grids):
        kind, part = divmod(g, parts)
        for core in range(2):
            pairs = []
            if kind == 0:
                own = [(i, j) for i in range(count) for j in range(i, count)]
                pairs += own[part::parts]
                for i in range(count):
                    for j in range(visitors):
                        if (i + j + part * visitors) % 2 == core:
                            pairs.append((i, count + j))
            else:
                pairs += [(i, count + j) for j in range(visitors) for i in range(count)]
            lists.append(pairs)
    longest = max(map(len, lists))
    batch = max(d for d in range(1, 10) if longest % d == 0)
    table = np.zeros((len(lists), longest, 4), np.int32)
    for row, pairs in enumerate(lists):
        for k, (a, b) in enumerate(pairs):
            table[row, k] = (a, b, 1, int(a != b))
    return table.reshape(grids, 2, longest * 4), longest, batch, parts, visitors


def routes(bands, grids, parts):
    moves = []
    for b in range(bands):
        for g in range(grids):
            chip, core = divmod(b, 2)
            other = chip ^ (g // parts)
            flip = 1 if other <= chip else 0
            source = other * 2 + (core ^ flip)
            moves.append((source * grids + g, b * grids + g))
    return moves


def high_low(values):
    high = values.astype(jnp.bfloat16)
    low = (values - high.astype(jnp.float32)).astype(jnp.bfloat16)
    return high, low


def exchange_kernel(
    batch, longest, pairs, weights, cutoff, own, visiting, planes, line, shells, screen,
    out_own, out_visiting, fields, outs, high, low, work,
):
    count, extent, cells = own.shape
    visitors = visiting.shape[0]
    half = cells // 2
    fields[:count] = own[...]
    fields[count:] = visiting[...]
    outs[...] = jnp.zeros_like(outs)

    def run_batch(step, _):
        def form(p, _):
            k = (step * batch + p) * 4
            a, b = pairs[k], pairs[k + 1]
            rows = pl.ds(pl.multiple_of(p * extent, extent), extent)
            near = fields[a, :, :half] * fields[b, :, :half]
            far = fields[a, :, half:] * fields[b, :, half:]
            for e, folded in enumerate((near + far, near - far)):
                high[e, rows, :], low[e, rows, :] = high_low(folded)
            return 0

        lax.fori_loop(0, batch, form, 0)

        def forward(e, _):
            total = jnp.dot(low[e], planes[e, 0], preferred_element_type=jnp.float32)
            total += jnp.dot(high[e], planes[e, 1], preferred_element_type=jnp.float32)
            total += jnp.dot(high[e], planes[e, 0], preferred_element_type=jnp.float32)
            work[e] = total
            return 0

        lax.fori_loop(0, 2, forward, 0)

        def screened(p, _):
            rows = pl.ds(pl.multiple_of(p * extent, extent), extent)
            for e in range(2):
                lanes = pl.ds(e * half, half)
                h, l = high_low(work[e, rows, :])
                spectrum = jnp.dot(
                    line[...], jnp.concatenate([h, l, h], axis=0),
                    preferred_element_type=jnp.float32,
                )
                factor = jnp.where(shells[:, lanes] <= cutoff[0], screen[:, lanes], 0.0)
                h, l = high_low(spectrum * factor)
                back = jnp.dot(
                    line[...], jnp.concatenate([h, l, h], axis=0),
                    preferred_element_type=jnp.float32,
                )
                high[e, rows, :], low[e, rows, :] = high_low(back)
            return 0

        lax.fori_loop(0, batch, screened, 0)

        def inverse(e, _):
            def product(left, right):
                return lax.dot_general(
                    left, right, (((1,), (1,)), ((), ())), preferred_element_type=jnp.float32
                )

            total = product(low[e], planes[e, 0])
            total += product(high[e], planes[e, 1])
            total += product(high[e], planes[e, 0])
            work[e] = total
            return 0

        lax.fori_loop(0, 2, inverse, 0)

        def apply(p, _):
            k = (step * batch + p) * 4
            a, b = pairs[k], pairs[k + 1]
            rows = pl.ds(pl.multiple_of(p * extent, extent), extent)
            to_a = -weights[b] * pairs[k + 2].astype(jnp.float32)
            to_b = -weights[a] * pairs[k + 3].astype(jnp.float32)
            even, odd = work[0, rows, :], work[1, rows, :]
            for lanes, v in ((pl.ds(0, half), even + odd), (pl.ds(half, half), even - odd)):
                phi_a, phi_b = fields[a, :, lanes], fields[b, :, lanes]
                outs[a, :, lanes] = outs[a, :, lanes] + to_a * (phi_b * v)
                outs[b, :, lanes] = outs[b, :, lanes] + to_b * (phi_a * v)
            return 0

        lax.fori_loop(0, batch, apply, 0)
        return 0

    lax.fori_loop(0, longest // batch, run_batch, 0)
    out_own[...] = outs[:count]
    out_visiting[...] = outs[count:]


def on_device(bands, grids, orbitals, occupation, cutoff):
    count, thickness, cells = orbitals.shape
    extent = thickness * grids
    planes, line, shells, screen = transform_tables(extent)
    table, longest, batch, parts, visitors = pair_lists(bands, grids, count)
    moves = routes(bands, grids, parts)
    back = [(d, s) for s, d in moves]
    axes = ("band", "grid")
    g = lax.axis_index("grid")
    core = lax.axis_index("band") % 2
    first = g % parts * visitors

    weights = occupation.astype(jnp.float32) * 0.5
    own = lax.all_gather(orbitals, "grid", axis=1, tiled=True)
    sent = own if parts == 1 else lax.dynamic_slice_in_dim(own, first, visitors, 0)
    sent_weights = weights if parts == 1 else lax.dynamic_slice_in_dim(weights, first, visitors, 0)
    visiting = lax.ppermute(sent, axes, moves)
    visiting_weights = lax.ppermute(sent_weights, axes, moves)
    all_weights = jnp.concatenate([weights, visiting_weights])
    pairs = jnp.asarray(table)[g, core]

    rows = batch * extent
    smem = pl.BlockSpec(memory_space=pltpu.SMEM)
    vmem = pl.BlockSpec(memory_space=pltpu.VMEM)
    slots = count + visitors
    out_own, out_visiting = pl.pallas_call(
        functools.partial(exchange_kernel, batch, longest),
        out_shape=(
            jax.ShapeDtypeStruct(own.shape, jnp.float32),
            jax.ShapeDtypeStruct(visiting.shape, jnp.float32),
        ),
        in_specs=[smem] * 3 + [vmem] * 6,
        out_specs=(vmem, vmem),
        scratch_shapes=[
            pltpu.VMEM((slots, extent, cells), jnp.float32),
            pltpu.VMEM((slots, extent, cells), jnp.float32),
            pltpu.VMEM((2, rows, cells // 2), jnp.bfloat16),
            pltpu.VMEM((2, rows, cells // 2), jnp.bfloat16),
            pltpu.VMEM((2, rows, cells // 2), jnp.float32),
        ],
        compiler_params=pltpu.CompilerParams(vmem_limit_bytes=56 * 1024 * 1024),
    )(
        pairs, all_weights, cutoff.reshape(1), own, visiting,
        jnp.asarray(planes), jnp.asarray(line), jnp.asarray(shells), jnp.asarray(screen),
    )
    returned = lax.ppermute(out_visiting, axes, back)
    if parts == 1:
        total = out_own + returned
    else:
        near = lax.dynamic_slice_in_dim(out_own, first, visitors, 0) + returned
        total = lax.dynamic_update_slice_in_dim(out_own, near, first, 0)
    return lax.psum_scatter(total, "grid", scatter_dimension=1, tiled=True)


def solution(mesh):
    placed = (P("band", "grid", None), P("band"), P())
    return jax.shard_map(
        functools.partial(on_device, mesh.shape["band"], mesh.shape["grid"]),
        mesh=mesh, in_specs=placed, out_specs=P("band", "grid", None), check_vma=False,
    )
```

```python
import functools

import jax
import jax.numpy as jnp
import ml_dtypes
import numpy as np
from jax import lax
from jax.experimental import pallas as pl
from jax.experimental.pallas import tpu as pltpu
from jax.sharding import PartitionSpec as P

screen_alpha = 2.0
screen_scale = 4.0


def split_halves(table):
    high = table.astype(ml_dtypes.bfloat16)
    low = (table - high.astype(np.float64)).astype(ml_dtypes.bfloat16)
    return high, low


@functools.cache
def transform_tables(extent):
    half = extent // 2
    position = np.arange(extent)
    angles = 2.0 * np.pi / extent * (position[:, None] * position[None, :] % extent)
    cas = np.cos(angles) + np.sin(angles)
    planes = [split_halves(np.kron(cas[:half, e::2], cas)) for e in (0, 1)]
    plane_tables = np.stack([np.stack(p) for p in planes])
    high, low = split_halves(cas)
    line_table = np.concatenate([high, high, low], axis=1)
    signed = np.where(position <= half, position, position - extent) ** 2
    order = np.concatenate([position[0::2], position[1::2]])
    shells = signed[:, None, None] + signed[order][None, :, None] + signed[None, None, :]
    shells = shells.reshape(extent, extent * extent).astype(np.int32)
    ratios = shells / screen_alpha
    screen = np.where(shells > 0, (1.0 - np.exp(-ratios)) / np.maximum(ratios, 0.1), 1.0)
    screen = (screen * (screen_scale / extent**3)).astype(np.float32)
    return plane_tables, line_table, shells, screen


@functools.cache
def pair_lists(bands, grids, count):
    chips = bands // 2
    parts = max(1, grids // chips)
    assert chips * parts == grids and count % parts == 0
    visitors = count // parts
    lists = []
    for g in range(grids):
        kind, part = divmod(g, parts)
        for core in range(2):
            pairs = []
            if kind == 0:
                own = [(i, j) for i in range(count) for j in range(i, count)]
                pairs += own[part::parts]
                for i in range(count):
                    for j in range(part * visitors, part * visitors + visitors):
                        if (i + j) % 2 == core:
                            pairs.append((i, count + j))
            else:
                kept = range(part * visitors, part * visitors + visitors)
                pairs += [(i, count + j) for j in kept for i in range(count)]
            lists.append(pairs)
    longest = max(map(len, lists))
    batch = max(d for d in range(1, 10) if longest % d == 0)
    table = np.zeros((len(lists), longest, 4), np.int32)
    for row, pairs in enumerate(lists):
        for k, (a, b) in enumerate(pairs):
            table[row, k] = (a, b, 1, int(a != b))
    return table.reshape(grids, 2, longest * 4), longest, batch, parts


def partners(bands, parts):
    band, g = lax.axis_index("band"), lax.axis_index("grid")
    chip, core, kind = band // 2, band % 2, g // parts
    other = 0
    bit = 1
    while bit < bands // 2:
        other += (chip // bit % 2 + kind // bit % 2) % 2 * bit
        bit *= 2
    source_flip = jnp.where(other <= chip, 1, 0)
    target_flip = jnp.where(chip <= other, 1, 0)
    return other * 2 + (core + source_flip) % 2, other * 2 + (core + target_flip) % 2


MESH = pl.DeviceIdType.MESH


def greet(z, grids, source, target):
    barrier = pltpu.get_barrier_semaphore()

    @pl.when(z > 0)
    def _():
        pl.semaphore_signal(barrier, inc=1, device_id={"grid": z - 1}, device_id_type=MESH)

    @pl.when(z < grids - 1)
    def _():
        pl.semaphore_signal(barrier, inc=1, device_id={"grid": z + 1}, device_id_type=MESH)

    pl.semaphore_signal(barrier, inc=1, device_id={"band": source}, device_id_type=MESH)
    pl.semaphore_signal(barrier, inc=1, device_id={"band": target}, device_id_type=MESH)
    pl.semaphore_wait(barrier, 2 + jnp.where(z > 0, 1, 0) + jnp.where(z < grids - 1, 1, 0))


def gather_kernel(
    bands, grids, parts, slab, own, visiting,
    local_sem, up_send, down_send, z_recv, visit_send, visit_recv,
):
    thickness = slab.shape[0]
    z = lax.axis_index("grid")
    source, target = partners(bands, parts)
    greet(z, grids, source, target)

    def part(ref, t):
        return ref.at[pl.ds(t * thickness, thickness)]

    def along(t, step, send, to):
        from_ref = slab if step == 0 else part(own, t)
        return pltpu.make_async_remote_copy(
            src_ref=from_ref, dst_ref=part(own, t), send_sem=send.at[step],
            recv_sem=z_recv.at[t], device_id={"grid": to}, device_id_type=MESH,
        )

    def visit(t, mine):
        return pltpu.make_async_remote_copy(
            src_ref=slab if mine else part(own, t), dst_ref=part(visiting, t),
            send_sem=visit_send.at[t], recv_sem=visit_recv.at[t],
            device_id={"band": target}, device_id_type=MESH,
        )

    def climbs(step):
        return (z >= step) & (z < grids - 1)

    def falls(step):
        return (z + step < grids) & (z > 0)

    keep = pltpu.make_async_copy(slab, part(own, z), local_sem)
    for step in range(grids):
        below, above = z - step, z + step
        if step > 0:
            @pl.when(below >= 0)
            def _():
                along(below, step, up_send, z).wait_recv()

            @pl.when(above < grids)
            def _():
                along(above, step, down_send, z).wait_recv()

        if step < grids - 1:
            @pl.when(climbs(step))
            def _():
                along(below, step, up_send, z + 1).start()

            @pl.when(falls(step))
            def _():
                along(above, step, down_send, z - 1).start()

        if step == 0:
            visit(z, True).start()
            keep.start()
        else:
            @pl.when(below >= 0)
            def _():
                visit(below, False).start()

            @pl.when(above < grids)
            def _():
                visit(above, False).start()

    for step in range(grids - 1):
        @pl.when(climbs(step))
        def _():
            along(z - step, step, up_send, z + 1).wait_send()

        @pl.when(falls(step))
        def _():
            along(z + step, step, down_send, z - 1).wait_send()

    keep.wait()
    for t in range(grids):
        visit(t, False).wait_send()
        visit(t, False).wait_recv()


def reduce_kernel(
    bands, grids, parts, own, visiting, out, returned, up_in, down_in, up_out, down_out,
    back_send, back_recv, up_send, up_recv, down_send, down_recv,
):
    thickness = out.shape[0]
    z = lax.axis_index("grid")
    source, target = partners(bands, parts)
    greet(z, grids, source, target)

    def rows(t):
        return pl.ds(t * thickness, thickness)

    def back(t):
        return pltpu.make_async_remote_copy(
            src_ref=visiting.at[rows(t)], dst_ref=returned.at[rows(t)],
            send_sem=back_send.at[t], recv_sem=back_recv.at[t],
            device_id={"band": source}, device_id_type=MESH,
        )

    def up(step):
        return pltpu.make_async_remote_copy(
            src_ref=up_out.at[step], dst_ref=up_in.at[step], send_sem=up_send.at[step],
            recv_sem=up_recv.at[step], device_id={"grid": z + 1}, device_id_type=MESH,
        )

    def down(step):
        return pltpu.make_async_remote_copy(
            src_ref=down_out.at[step], dst_ref=down_in.at[step], send_sem=down_send.at[step],
            recv_sem=down_recv.at[step], device_id={"grid": z - 1}, device_id_type=MESH,
        )

    for o in range(grids):
        back(jnp.where(z < grids // 2, grids - 1 - o, o)).start()
    last = grids - 1
    for step in range(grids - 1):
        for copy, inbox, outbox, z_from, t in (
            (up, up_in, up_out, z, last - step + z),
            (down, down_in, down_out, last - z, step - last + z),
        ):
            @pl.when(z_from <= step)
            def _():
                back(t).wait_recv()
                outbox[step] = own[rows(t)] + returned[rows(t)]
                if step > 0:
                    @pl.when(z_from >= 1)
                    def _():
                        copy(step - 1).wait_recv()
                        outbox[step] = outbox[step] + inbox[step - 1]
                copy(step).start()

    back(z).wait_recv()
    out[...] = own[rows(z)] + returned[rows(z)]

    @pl.when(z >= 1)
    def _():
        up(last - 1).wait_recv()
        out[...] = out[...] + up_in[last - 1]

    @pl.when(z < last)
    def _():
        down(last - 1).wait_recv()
        out[...] = out[...] + down_in[last - 1]

    for step in range(grids - 1):
        @pl.when(z <= step)
        def _():
            up(step).wait_send()

        @pl.when(last - z <= step)
        def _():
            down(step).wait_send()

    for t in range(grids):
        back(t).wait_send()


def high_low(values):
    high = values.astype(jnp.bfloat16)
    low = (values - high.astype(jnp.float32)).astype(jnp.bfloat16)
    return high, low


def exchange_kernel(
    batch, longest, pairs, weights, cutoff, own, visiting, planes, line, shells, screen,
    out_own, out_visiting, fields, outs, high, low, work,
):
    count, extent, cells = own.shape
    visitors = visiting.shape[0]
    half = cells // 2
    fields[:count] = own[...]
    fields[count:] = visiting[...]
    outs[...] = jnp.zeros_like(outs)

    def run_batch(step, _):
        def form(p, _):
            k = (step * batch + p) * 4
            a, b = pairs[k], pairs[k + 1]
            rows = pl.ds(pl.multiple_of(p * extent, extent), extent)
            near = fields[a, :, :half] * fields[b, :, :half]
            far = fields[a, :, half:] * fields[b, :, half:]
            for e, folded in enumerate((near + far, near - far)):
                high[e, rows, :], low[e, rows, :] = high_low(folded)
            return 0

        lax.fori_loop(0, batch, form, 0)

        def forward(e, _):
            total = jnp.dot(low[e], planes[e, 0], preferred_element_type=jnp.float32)
            total += jnp.dot(high[e], planes[e, 1], preferred_element_type=jnp.float32)
            total += jnp.dot(high[e], planes[e, 0], preferred_element_type=jnp.float32)
            work[e] = total
            return 0

        lax.fori_loop(0, 2, forward, 0)

        def screened(p, _):
            rows = pl.ds(pl.multiple_of(p * extent, extent), extent)
            for e in range(2):
                lanes = pl.ds(e * half, half)
                h, l = high_low(work[e, rows, :])
                spectrum = jnp.dot(
                    line[...], jnp.concatenate([h, l, h], axis=0),
                    preferred_element_type=jnp.float32,
                )
                factor = jnp.where(shells[:, lanes] <= cutoff[0], screen[:, lanes], 0.0)
                h, l = high_low(spectrum * factor)
                back = jnp.dot(
                    line[...], jnp.concatenate([h, l, h], axis=0),
                    preferred_element_type=jnp.float32,
                )
                high[e, rows, :], low[e, rows, :] = high_low(back)
            return 0

        lax.fori_loop(0, batch, screened, 0)

        def inverse(e, _):
            def product(left, right):
                return lax.dot_general(
                    left, right, (((1,), (1,)), ((), ())), preferred_element_type=jnp.float32
                )

            total = product(low[e], planes[e, 0])
            total += product(high[e], planes[e, 1])
            total += product(high[e], planes[e, 0])
            work[e] = total
            return 0

        lax.fori_loop(0, 2, inverse, 0)

        def apply(p, _):
            k = (step * batch + p) * 4
            a, b = pairs[k], pairs[k + 1]
            rows = pl.ds(pl.multiple_of(p * extent, extent), extent)
            to_a = -weights[b] * pairs[k + 2].astype(jnp.float32)
            to_b = -weights[a] * pairs[k + 3].astype(jnp.float32)
            even, odd = work[0, rows, :], work[1, rows, :]
            for lanes, v in ((pl.ds(0, half), even + odd), (pl.ds(half, half), even - odd)):
                phi_a, phi_b = fields[a, :, lanes], fields[b, :, lanes]
                outs[a, :, lanes] = outs[a, :, lanes] + to_a * (phi_b * v)
                outs[b, :, lanes] = outs[b, :, lanes] + to_b * (phi_a * v)
            return 0

        lax.fori_loop(0, batch, apply, 0)
        return 0

    lax.fori_loop(0, longest // batch, run_batch, 0)
    out_own[...] = outs[:count]
    out_visiting[...] = outs[count:]


def on_device(bands, grids, orbitals, occupation, cutoff):
    count, thickness, cells = orbitals.shape
    extent = thickness * grids
    planes, line, shells, screen = transform_tables(extent)
    table, longest, batch, parts = pair_lists(bands, grids, count)
    g = lax.axis_index("grid")
    band = lax.axis_index("band")
    weights = occupation.astype(jnp.float32) * 0.5
    every_weight = lax.all_gather(weights, "band", axis=0)
    source, _ = partners(bands, parts)
    all_weights = jnp.concatenate([weights, every_weight[source]])
    pairs = jnp.asarray(table)[g, band % 2]

    anywhere = pl.BlockSpec(memory_space=pl.ANY)
    dma = pltpu.SemaphoreType.DMA
    whole = jax.ShapeDtypeStruct((extent, count, cells), jnp.float32)
    gathered = pl.pallas_call(
        functools.partial(gather_kernel, bands, grids, parts),
        out_shape=(whole, whole),
        in_specs=[anywhere],
        out_specs=(anywhere, anywhere),
        scratch_shapes=[
            dma, dma((grids,)), dma((grids,)), dma((grids,)), dma((grids,)), dma((grids,)),
        ],
        compiler_params=pltpu.CompilerParams(collective_id=0, has_side_effects=True),
    )(orbitals.transpose(1, 0, 2))
    own, visiting = (x.transpose(1, 0, 2) for x in gathered)

    rows = batch * extent
    smem = pl.BlockSpec(memory_space=pltpu.SMEM)
    vmem = pl.BlockSpec(memory_space=pltpu.VMEM)
    slots = 2 * count
    out_own, out_visiting = pl.pallas_call(
        functools.partial(exchange_kernel, batch, longest),
        out_shape=(
            jax.ShapeDtypeStruct(own.shape, jnp.float32),
            jax.ShapeDtypeStruct(visiting.shape, jnp.float32),
        ),
        in_specs=[smem] * 3 + [vmem] * 6,
        out_specs=(vmem, vmem),
        scratch_shapes=[
            pltpu.VMEM((slots, extent, cells), jnp.float32),
            pltpu.VMEM((slots, extent, cells), jnp.float32),
            pltpu.VMEM((2, rows, cells // 2), jnp.bfloat16),
            pltpu.VMEM((2, rows, cells // 2), jnp.bfloat16),
            pltpu.VMEM((2, rows, cells // 2), jnp.float32),
        ],
        compiler_params=pltpu.CompilerParams(vmem_limit_bytes=56 * 1024 * 1024),
    )(
        pairs, all_weights, cutoff.reshape(1), own, visiting,
        jnp.asarray(planes), jnp.asarray(line), jnp.asarray(shells), jnp.asarray(screen),
    )
    steps = grids - 1
    slabs = pltpu.VMEM((steps, thickness, count, cells), jnp.float32)
    total = pl.pallas_call(
        functools.partial(reduce_kernel, bands, grids, parts),
        out_shape=jax.ShapeDtypeStruct((thickness, count, cells), jnp.float32),
        in_specs=[vmem, vmem],
        out_specs=vmem,
        scratch_shapes=[
            pltpu.VMEM((extent, count, cells), jnp.float32), slabs, slabs, slabs, slabs,
            dma((grids,)), dma((grids,)), dma((steps,)), dma((steps,)), dma((steps,)), dma((steps,)),
        ],
        compiler_params=pltpu.CompilerParams(
            collective_id=1, has_side_effects=True, vmem_limit_bytes=56 * 1024 * 1024
        ),
    )(out_own.transpose(1, 0, 2), out_visiting.transpose(1, 0, 2))
    return total.transpose(1, 0, 2)


def solution(mesh):
    placed = (P("band", "grid", None), P("band"), P())
    return jax.shard_map(
        functools.partial(on_device, mesh.shape["band"], mesh.shape["grid"]),
        mesh=mesh, in_specs=placed, out_specs=P("band", "grid", None), check_vma=False,
    )
```

```python
import functools

import jax
import jax.numpy as jnp
import ml_dtypes
import numpy as np
from jax import lax
from jax.experimental import pallas as pl
from jax.experimental.pallas import tpu as pltpu
from jax.sharding import PartitionSpec as P

screen_alpha = 2.0
screen_scale = 4.0


def split_halves(table):
    high = table.astype(ml_dtypes.bfloat16)
    low = (table - high.astype(np.float64)).astype(ml_dtypes.bfloat16)
    return high, low


@functools.cache
def transform_tables(extent):
    half = extent // 2
    position = np.arange(extent)
    angles = 2.0 * np.pi / extent * (position[:, None] * position[None, :] % extent)
    cas = np.cos(angles) + np.sin(angles)
    planes = [split_halves(np.kron(cas[:half, e::2], cas)) for e in (0, 1)]
    plane_tables = np.stack([np.stack(p) for p in planes])
    high, low = split_halves(cas)
    line_table = np.concatenate([high, high, low], axis=1)
    signed = np.where(position <= half, position, position - extent) ** 2
    order = np.concatenate([position[0::2], position[1::2]])
    shells = signed[:, None, None] + signed[order][None, :, None] + signed[None, None, :]
    shells = shells.reshape(extent, extent * extent).astype(np.int32)
    ratios = shells / screen_alpha
    screen = np.where(shells > 0, (1.0 - np.exp(-ratios)) / np.maximum(ratios, 0.1), 1.0)
    screen = (screen * (screen_scale / extent**3)).astype(np.float32)
    return plane_tables, line_table, shells, screen


@functools.cache
def pair_lists(bands, grids, count):
    chips = bands // 2
    parts = max(1, grids // chips)
    assert chips * parts == grids and count % parts == 0
    visitors = count // parts
    lists = []
    for g in range(grids):
        kind, part = divmod(g, parts)
        for core in range(2):
            pairs = []
            if kind == 0:
                own = [(i, j) for i in range(count) for j in range(i, count)]
                pairs += own[part::parts]
                for i in range(count):
                    for j in range(part * visitors, part * visitors + visitors):
                        if (i + j) % 2 == core:
                            pairs.append((i, count + j))
            else:
                kept = range(part * visitors, part * visitors + visitors)
                pairs += [(i, count + j) for j in kept for i in range(count)]
            lists.append(pairs)
    longest = max(map(len, lists))
    batch = max(d for d in range(1, 10) if longest % d == 0)
    table = np.zeros((len(lists), longest, 4), np.int32)
    for row, pairs in enumerate(lists):
        for k, (a, b) in enumerate(pairs):
            table[row, k] = (a, b, 1, int(a != b))
    return table.reshape(grids, 2, longest * 4), longest, batch, parts


def partners(bands, parts):
    band, g = lax.axis_index("band"), lax.axis_index("grid")
    chip, core, kind = band // 2, band % 2, g // parts
    other = 0
    bit = 1
    while bit < bands // 2:
        other += (chip // bit % 2 + kind // bit % 2) % 2 * bit
        bit *= 2
    source_flip = jnp.where(other <= chip, 1, 0)
    target_flip = jnp.where(chip <= other, 1, 0)
    return other * 2 + (core + source_flip) % 2, other * 2 + (core + target_flip) % 2


def routes(bands, grids, parts):
    moves = []
    for b in range(bands):
        for g in range(grids):
            chip, core = divmod(b, 2)
            other = chip ^ (g // parts)
            source = other * 2 + (core ^ int(other <= chip))
            moves.append((source * grids + g, b * grids + g))
    return moves


MESH = pl.DeviceIdType.MESH
CHUNKS = 2


def greet(z, grids, source, target):
    barrier = pltpu.get_barrier_semaphore()

    @pl.when(z > 0)
    def _():
        pl.semaphore_signal(barrier, inc=1, device_id={"grid": z - 1}, device_id_type=MESH)

    @pl.when(z < grids - 1)
    def _():
        pl.semaphore_signal(barrier, inc=1, device_id={"grid": z + 1}, device_id_type=MESH)

    pl.semaphore_signal(barrier, inc=1, device_id={"band": source}, device_id_type=MESH)
    pl.semaphore_signal(barrier, inc=1, device_id={"band": target}, device_id_type=MESH)
    pl.semaphore_wait(barrier, 2 + jnp.where(z > 0, 1, 0) + jnp.where(z < grids - 1, 1, 0))


def gather_kernel(
    bands, grids, parts, slab, own, visiting,
    local_sem, up_send, down_send, z_recv, visit_send, visit_recv,
):
    thickness = slab.shape[0]
    z = lax.axis_index("grid")
    source, target = partners(bands, parts)
    greet(z, grids, source, target)

    def part(ref, t):
        return ref.at[pl.ds(t * thickness, thickness)]

    def along(t, step, send, to):
        from_ref = slab if step == 0 else part(own, t)
        return pltpu.make_async_remote_copy(
            src_ref=from_ref, dst_ref=part(own, t), send_sem=send.at[step],
            recv_sem=z_recv.at[t], device_id={"grid": to}, device_id_type=MESH,
        )

    def visit(t, mine):
        return pltpu.make_async_remote_copy(
            src_ref=slab if mine else part(own, t), dst_ref=part(visiting, t),
            send_sem=visit_send.at[t], recv_sem=visit_recv.at[t],
            device_id={"band": target}, device_id_type=MESH,
        )

    def climbs(step):
        return (z >= step) & (z < grids - 1)

    def falls(step):
        return (z + step < grids) & (z > 0)

    keep = pltpu.make_async_copy(slab, part(own, z), local_sem)
    for step in range(grids):
        below, above = z - step, z + step
        if step > 0:
            @pl.when(below >= 0)
            def _():
                along(below, step, up_send, z).wait_recv()

            @pl.when(above < grids)
            def _():
                along(above, step, down_send, z).wait_recv()

        if step < grids - 1:
            @pl.when(climbs(step))
            def _():
                along(below, step, up_send, z + 1).start()

            @pl.when(falls(step))
            def _():
                along(above, step, down_send, z - 1).start()

        if step == 0:
            visit(z, True).start()
            keep.start()
        else:
            @pl.when(below >= 0)
            def _():
                visit(below, False).start()

            @pl.when(above < grids)
            def _():
                visit(above, False).start()

    for step in range(grids - 1):
        @pl.when(climbs(step))
        def _():
            along(z - step, step, up_send, z + 1).wait_send()

        @pl.when(falls(step))
        def _():
            along(z + step, step, down_send, z - 1).wait_send()

    keep.wait()
    for t in range(grids):
        visit(t, False).wait_send()
        visit(t, False).wait_recv()


def reduce_kernel(
    bands, grids, parts, own, visiting, out, returned, up_in, down_in, up_out, down_out,
    back_send, back_recv, up_send, up_recv, down_send, down_recv,
):
    thickness = out.shape[0]
    z = lax.axis_index("grid")
    source, target = partners(bands, parts)
    greet(z, grids, source, target)

    cells = out.shape[2] // CHUNKS
    last = grids - 1

    def rows(t):
        return pl.ds(t * thickness, thickness)

    def lanes(c):
        return pl.ds(c * cells, cells)

    def back(t, c):
        return pltpu.make_async_remote_copy(
            src_ref=visiting.at[rows(t), :, lanes(c)], dst_ref=returned.at[rows(t), :, lanes(c)],
            send_sem=back_send.at[t, c], recv_sem=back_recv.at[t, c],
            device_id={"band": source}, device_id_type=MESH,
        )

    def up(step, c):
        return pltpu.make_async_remote_copy(
            src_ref=up_out.at[step, :, :, lanes(c)], dst_ref=up_in.at[step, :, :, lanes(c)],
            send_sem=up_send.at[step, c], recv_sem=up_recv.at[step, c],
            device_id={"grid": z + 1}, device_id_type=MESH,
        )

    def down(step, c):
        return pltpu.make_async_remote_copy(
            src_ref=down_out.at[step, :, :, lanes(c)], dst_ref=down_in.at[step, :, :, lanes(c)],
            send_sem=down_send.at[step, c], recv_sem=down_recv.at[step, c],
            device_id={"grid": z - 1}, device_id_type=MESH,
        )

    def turn(i):
        o = i // CHUNKS
        return back(jnp.where(z < grids // 2, last - o, o), i % CHUNKS)

    turns = grids * CHUNKS
    for i in range(min(2, turns)):
        turn(i).start()
    for i in range(turns):
        turn(i).wait_send()
        if i + 2 < turns:
            turn(i + 2).start()
        step, c = divmod(i, CHUNKS)
        if step == last:
            continue
        for copy, inbox, outbox, z_from, t in (
            (up, up_in, up_out, z, last - step + z),
            (down, down_in, down_out, last - z, step - last + z),
        ):
            @pl.when(z_from <= step)
            def _():
                back(t, c).wait_recv()
                outbox[step, :, :, lanes(c)] = own[rows(t), :, lanes(c)] + returned[rows(t), :, lanes(c)]
                if step > 0:
                    @pl.when(z_from >= 1)
                    def _():
                        copy(step - 1, c).wait_recv()
                        outbox[step, :, :, lanes(c)] = (
                            outbox[step, :, :, lanes(c)] + inbox[step - 1, :, :, lanes(c)]
                        )
                copy(step, c).start()

    for c in range(CHUNKS):
        back(z, c).wait_recv()
        out[:, :, lanes(c)] = own[rows(z), :, lanes(c)] + returned[rows(z), :, lanes(c)]

        @pl.when(z >= 1)
        def _():
            up(last - 1, c).wait_recv()
            out[:, :, lanes(c)] = out[:, :, lanes(c)] + up_in[last - 1, :, :, lanes(c)]

        @pl.when(z < last)
        def _():
            down(last - 1, c).wait_recv()
            out[:, :, lanes(c)] = out[:, :, lanes(c)] + down_in[last - 1, :, :, lanes(c)]

    for step in range(grids - 1):
        for c in range(CHUNKS):
            @pl.when(z <= step)
            def _():
                up(step, c).wait_send()

            @pl.when(last - z <= step)
            def _():
                down(step, c).wait_send()


def high_low(values):
    high = values.astype(jnp.bfloat16)
    low = (values - high.astype(jnp.float32)).astype(jnp.bfloat16)
    return high, low


def exchange_kernel(
    batch, longest, pairs, weights, cutoff, own, visiting, planes, line, shells, screen,
    out_own, out_visiting, fields, outs, high, low, work,
):
    count, extent, cells = own.shape
    visitors = visiting.shape[0]
    half = cells // 2
    fields[:count] = own[...]
    fields[count:] = visiting[...]
    outs[...] = jnp.zeros_like(outs)

    def run_batch(step, _):
        def form(p, _):
            k = (step * batch + p) * 4
            a, b = pairs[k], pairs[k + 1]
            rows = pl.ds(pl.multiple_of(p * extent, extent), extent)
            near = fields[a, :, :half] * fields[b, :, :half]
            far = fields[a, :, half:] * fields[b, :, half:]
            for e, folded in enumerate((near + far, near - far)):
                high[e, rows, :], low[e, rows, :] = high_low(folded)
            return 0

        lax.fori_loop(0, batch, form, 0)

        def forward(e, _):
            total = jnp.dot(low[e], planes[e, 0], preferred_element_type=jnp.float32)
            total += jnp.dot(high[e], planes[e, 1], preferred_element_type=jnp.float32)
            total += jnp.dot(high[e], planes[e, 0], preferred_element_type=jnp.float32)
            work[e] = total
            return 0

        lax.fori_loop(0, 2, forward, 0)

        def screened(p, _):
            rows = pl.ds(pl.multiple_of(p * extent, extent), extent)
            for e in range(2):
                lanes = pl.ds(e * half, half)
                h, l = high_low(work[e, rows, :])
                spectrum = jnp.dot(
                    line[...], jnp.concatenate([h, l, h], axis=0),
                    preferred_element_type=jnp.float32,
                )
                factor = jnp.where(shells[:, lanes] <= cutoff[0], screen[:, lanes], 0.0)
                h, l = high_low(spectrum * factor)
                back = jnp.dot(
                    line[...], jnp.concatenate([h, l, h], axis=0),
                    preferred_element_type=jnp.float32,
                )
                high[e, rows, :], low[e, rows, :] = high_low(back)
            return 0

        lax.fori_loop(0, batch, screened, 0)

        def inverse(e, _):
            def product(left, right):
                return lax.dot_general(
                    left, right, (((1,), (1,)), ((), ())), preferred_element_type=jnp.float32
                )

            total = product(low[e], planes[e, 0])
            total += product(high[e], planes[e, 1])
            total += product(high[e], planes[e, 0])
            work[e] = total
            return 0

        lax.fori_loop(0, 2, inverse, 0)

        def apply(p, _):
            k = (step * batch + p) * 4
            a, b = pairs[k], pairs[k + 1]
            rows = pl.ds(pl.multiple_of(p * extent, extent), extent)
            to_a = -weights[b] * pairs[k + 2].astype(jnp.float32)
            to_b = -weights[a] * pairs[k + 3].astype(jnp.float32)
            even, odd = work[0, rows, :], work[1, rows, :]
            for lanes, v in ((pl.ds(0, half), even + odd), (pl.ds(half, half), even - odd)):
                phi_a, phi_b = fields[a, :, lanes], fields[b, :, lanes]
                outs[a, :, lanes] = outs[a, :, lanes] + to_a * (phi_b * v)
                outs[b, :, lanes] = outs[b, :, lanes] + to_b * (phi_a * v)
            return 0

        lax.fori_loop(0, batch, apply, 0)
        return 0

    lax.fori_loop(0, longest // batch, run_batch, 0)
    out_own[...] = outs[:count]
    out_visiting[...] = outs[count:]


def on_device(bands, grids, orbitals, occupation, cutoff):
    count, thickness, cells = orbitals.shape
    extent = thickness * grids
    planes, line, shells, screen = transform_tables(extent)
    table, longest, batch, parts = pair_lists(bands, grids, count)
    g = lax.axis_index("grid")
    band = lax.axis_index("band")
    weights = occupation.astype(jnp.float32) * 0.5
    visiting_weights = lax.ppermute(weights, ("band", "grid"), routes(bands, grids, parts))
    all_weights = jnp.concatenate([weights, visiting_weights])
    pairs = jnp.asarray(table)[g, band % 2]

    anywhere = pl.BlockSpec(memory_space=pl.ANY)
    dma = pltpu.SemaphoreType.DMA
    whole = jax.ShapeDtypeStruct((extent, count, cells), jnp.float32)
    gathered = pl.pallas_call(
        functools.partial(gather_kernel, bands, grids, parts),
        out_shape=(whole, whole),
        in_specs=[anywhere],
        out_specs=(anywhere, anywhere),
        scratch_shapes=[
            dma, dma((grids,)), dma((grids,)), dma((grids,)), dma((grids,)), dma((grids,)),
        ],
        compiler_params=pltpu.CompilerParams(collective_id=0, has_side_effects=True),
    )(orbitals.transpose(1, 0, 2))
    own, visiting = (x.transpose(1, 0, 2) for x in gathered)

    rows = batch * extent
    smem = pl.BlockSpec(memory_space=pltpu.SMEM)
    vmem = pl.BlockSpec(memory_space=pltpu.VMEM)
    slots = 2 * count
    out_own, out_visiting = pl.pallas_call(
        functools.partial(exchange_kernel, batch, longest),
        out_shape=(
            jax.ShapeDtypeStruct(own.shape, jnp.float32),
            jax.ShapeDtypeStruct(visiting.shape, jnp.float32),
        ),
        in_specs=[smem] * 3 + [vmem] * 6,
        out_specs=(vmem, vmem),
        scratch_shapes=[
            pltpu.VMEM((slots, extent, cells), jnp.float32),
            pltpu.VMEM((slots, extent, cells), jnp.float32),
            pltpu.VMEM((2, rows, cells // 2), jnp.bfloat16),
            pltpu.VMEM((2, rows, cells // 2), jnp.bfloat16),
            pltpu.VMEM((2, rows, cells // 2), jnp.float32),
        ],
        compiler_params=pltpu.CompilerParams(vmem_limit_bytes=56 * 1024 * 1024),
    )(
        pairs, all_weights, cutoff.reshape(1), own, visiting,
        jnp.asarray(planes), jnp.asarray(line), jnp.asarray(shells), jnp.asarray(screen),
    )
    steps = grids - 1
    slabs = pltpu.VMEM((steps, thickness, count, cells), jnp.float32)
    total = pl.pallas_call(
        functools.partial(reduce_kernel, bands, grids, parts),
        out_shape=jax.ShapeDtypeStruct((thickness, count, cells), jnp.float32),
        in_specs=[vmem, vmem],
        out_specs=vmem,
        scratch_shapes=[
            pltpu.VMEM((extent, count, cells), jnp.float32), slabs, slabs, slabs, slabs,
            *[dma((grids, CHUNKS))] * 2, *[dma((steps, CHUNKS))] * 4,
        ],
        compiler_params=pltpu.CompilerParams(
            collective_id=1, has_side_effects=True, vmem_limit_bytes=56 * 1024 * 1024
        ),
    )(out_own.transpose(1, 0, 2), out_visiting.transpose(1, 0, 2))
    return total.transpose(1, 0, 2)


def solution(mesh):
    placed = (P("band", "grid", None), P("band"), P())
    return jax.shard_map(
        functools.partial(on_device, mesh.shape["band"], mesh.shape["grid"]),
        mesh=mesh, in_specs=placed, out_specs=P("band", "grid", None), check_vma=False,
    )
```

```python
import functools

import jax
import jax.numpy as jnp
import ml_dtypes
import numpy as np
from jax import lax
from jax.experimental import pallas as pl
from jax.experimental.pallas import tpu as pltpu
from jax.sharding import PartitionSpec as P

screen_alpha = 2.0
screen_scale = 4.0


def split_halves(table):
    high = table.astype(ml_dtypes.bfloat16)
    low = (table - high.astype(np.float64)).astype(ml_dtypes.bfloat16)
    return high, low


@functools.cache
def transform_tables(extent):
    half = extent // 2
    position = np.arange(extent)
    angles = 2.0 * np.pi / extent * (position[:, None] * position[None, :] % extent)
    cas = np.cos(angles) + np.sin(angles)
    planes = [split_halves(np.kron(cas[:half, e::2], cas)) for e in (0, 1)]
    plane_tables = np.stack([np.stack(p) for p in planes])
    high, low = split_halves(cas)
    line_table = np.concatenate([high, high, low], axis=1)
    signed = np.where(position <= half, position, position - extent) ** 2
    order = np.concatenate([position[0::2], position[1::2]])
    shells = signed[:, None, None] + signed[order][None, :, None] + signed[None, None, :]
    shells = shells.reshape(extent, extent * extent).astype(np.int32)
    ratios = shells / screen_alpha
    screen = np.where(shells > 0, (1.0 - np.exp(-ratios)) / np.maximum(ratios, 0.1), 1.0)
    screen = (screen * (screen_scale / extent**3)).astype(np.float32)
    return plane_tables, line_table, shells, screen


@functools.cache
def pair_lists(bands, grids, count):
    chips = bands // 2
    parts = max(1, grids // chips)
    assert chips * parts == grids and count % parts == 0
    visitors = count // parts
    lists = []
    for g in range(grids):
        kind, part = divmod(g, parts)
        for core in range(2):
            pairs = []
            if kind == 0:
                own = [(i, j) for i in range(count) for j in range(i, count)]
                pairs += own[part::parts]
                for i in range(count):
                    for j in range(part * visitors, part * visitors + visitors):
                        if (i + j) % 2 == core:
                            pairs.append((i, count + j))
            else:
                kept = range(part * visitors, part * visitors + visitors)
                pairs += [(i, count + j) for j in kept for i in range(count)]
            lists.append(pairs)
    longest = max(map(len, lists))
    batch = max(d for d in range(1, 10) if longest % d == 0)
    table = np.zeros((len(lists), longest, 4), np.int32)
    for row, pairs in enumerate(lists):
        for k, (a, b) in enumerate(pairs):
            table[row, k] = (a, b, 1, int(a != b))
    return table.reshape(grids, 2, longest * 4), longest, batch, parts


def partners(bands, parts):
    band, g = lax.axis_index("band"), lax.axis_index("grid")
    chip, core, kind = band // 2, band % 2, g // parts
    other = 0
    bit = 1
    while bit < bands // 2:
        other += (chip // bit % 2 + kind // bit % 2) % 2 * bit
        bit *= 2
    source_flip = jnp.where(other <= chip, 1, 0)
    target_flip = jnp.where(chip <= other, 1, 0)
    return other * 2 + (core + source_flip) % 2, other * 2 + (core + target_flip) % 2


def routes(bands, grids, parts):
    moves = []
    for b in range(bands):
        for g in range(grids):
            chip, core = divmod(b, 2)
            other = chip ^ (g // parts)
            source = other * 2 + (core ^ int(other <= chip))
            moves.append((source * grids + g, b * grids + g))
    return moves


MESH = pl.DeviceIdType.MESH
CHUNKS = 2


def greet(z, grids, source, target):
    barrier = pltpu.get_barrier_semaphore()

    @pl.when(z > 0)
    def _():
        pl.semaphore_signal(barrier, inc=1, device_id={"grid": z - 1}, device_id_type=MESH)

    @pl.when(z < grids - 1)
    def _():
        pl.semaphore_signal(barrier, inc=1, device_id={"grid": z + 1}, device_id_type=MESH)

    pl.semaphore_signal(barrier, inc=1, device_id={"band": source}, device_id_type=MESH)
    pl.semaphore_signal(barrier, inc=1, device_id={"band": target}, device_id_type=MESH)
    pl.semaphore_wait(barrier, 2 + jnp.where(z > 0, 1, 0) + jnp.where(z < grids - 1, 1, 0))


def gather_kernel(
    bands, grids, parts, slab, own, visiting,
    local_sem, up_send, down_send, z_recv, visit_send, visit_recv,
):
    thickness = slab.shape[0]
    z = lax.axis_index("grid")
    source, target = partners(bands, parts)
    greet(z, grids, source, target)

    def part(ref, t):
        return ref.at[pl.ds(t * thickness, thickness)]

    def along(t, step, send, to):
        from_ref = slab if step == 0 else part(own, t)
        return pltpu.make_async_remote_copy(
            src_ref=from_ref, dst_ref=part(own, t), send_sem=send.at[step],
            recv_sem=z_recv.at[t], device_id={"grid": to}, device_id_type=MESH,
        )

    def visit(t, mine):
        return pltpu.make_async_remote_copy(
            src_ref=slab if mine else part(own, t), dst_ref=part(visiting, t),
            send_sem=visit_send.at[t], recv_sem=visit_recv.at[t],
            device_id={"band": target}, device_id_type=MESH,
        )

    def climbs(step):
        return (z >= step) & (z < grids - 1)

    def falls(step):
        return (z + step < grids) & (z > 0)

    keep = pltpu.make_async_copy(slab, part(own, z), local_sem)
    for step in range(grids):
        below, above = z - step, z + step
        if step > 0:
            @pl.when(below >= 0)
            def _():
                along(below, step, up_send, z).wait_recv()

            @pl.when(above < grids)
            def _():
                along(above, step, down_send, z).wait_recv()

        if step < grids - 1:
            @pl.when(climbs(step))
            def _():
                along(below, step, up_send, z + 1).start()

            @pl.when(falls(step))
            def _():
                along(above, step, down_send, z - 1).start()

        if step == 0:
            visit(z, True).start()
            keep.start()
        else:
            @pl.when(below >= 0)
            def _():
                visit(below, False).start()

            @pl.when(above < grids)
            def _():
                visit(above, False).start()

    for step in range(grids - 1):
        @pl.when(climbs(step))
        def _():
            along(z - step, step, up_send, z + 1).wait_send()

        @pl.when(falls(step))
        def _():
            along(z + step, step, down_send, z - 1).wait_send()

    keep.wait()
    for t in range(grids):
        visit(t, False).wait_send()
        visit(t, False).wait_recv()


def reduce_kernel(
    bands, grids, parts, own, visiting, out, returned, up_in, down_in, up_out, down_out,
    back_send, back_recv, up_send, up_recv, down_send, down_recv,
):
    thickness = out.shape[0]
    z = lax.axis_index("grid")
    source, target = partners(bands, parts)
    greet(z, grids, source, target)

    cells = out.shape[2] // CHUNKS
    last = grids - 1

    def rows(t):
        return pl.ds(t * thickness, thickness)

    def lanes(c):
        return pl.ds(c * cells, cells)

    def back(t, c):
        return pltpu.make_async_remote_copy(
            src_ref=visiting.at[rows(t), :, lanes(c)], dst_ref=returned.at[rows(t), :, lanes(c)],
            send_sem=back_send.at[t, c], recv_sem=back_recv.at[t, c],
            device_id={"band": source}, device_id_type=MESH,
        )

    def up(step, c):
        return pltpu.make_async_remote_copy(
            src_ref=up_out.at[step, :, :, lanes(c)], dst_ref=up_in.at[step, :, :, lanes(c)],
            send_sem=up_send.at[step, c], recv_sem=up_recv.at[step, c],
            device_id={"grid": z + 1}, device_id_type=MESH,
        )

    def down(step, c):
        return pltpu.make_async_remote_copy(
            src_ref=down_out.at[step, :, :, lanes(c)], dst_ref=down_in.at[step, :, :, lanes(c)],
            send_sem=down_send.at[step, c], recv_sem=down_recv.at[step, c],
            device_id={"grid": z - 1}, device_id_type=MESH,
        )

    def turn(i):
        o = i // CHUNKS
        t = jnp.where(z < grids // 2, (z + last - o) % grids, (z + 1 + o) % grids)
        return back(t, i % CHUNKS)

    turns = grids * CHUNKS
    for i in range(min(2, turns)):
        turn(i).start()
    for i in range(turns):
        turn(i).wait_send()
        if i + 2 < turns:
            turn(i + 2).start()
        step, c = divmod(i, CHUNKS)
        if step == last:
            continue
        for copy, inbox, outbox, z_from, t in (
            (up, up_in, up_out, z, last - step + z),
            (down, down_in, down_out, last - z, step - last + z),
        ):
            @pl.when(z_from <= step)
            def _():
                back(t, c).wait_recv()
                outbox[step, :, :, lanes(c)] = own[rows(t), :, lanes(c)] + returned[rows(t), :, lanes(c)]
                if step > 0:
                    @pl.when(z_from >= 1)
                    def _():
                        copy(step - 1, c).wait_recv()
                        outbox[step, :, :, lanes(c)] = (
                            outbox[step, :, :, lanes(c)] + inbox[step - 1, :, :, lanes(c)]
                        )
                copy(step, c).start()

    for c in range(CHUNKS):
        back(z, c).wait_recv()
        out[:, :, lanes(c)] = own[rows(z), :, lanes(c)] + returned[rows(z), :, lanes(c)]

        @pl.when(z >= 1)
        def _():
            up(last - 1, c).wait_recv()
            out[:, :, lanes(c)] = out[:, :, lanes(c)] + up_in[last - 1, :, :, lanes(c)]

        @pl.when(z < last)
        def _():
            down(last - 1, c).wait_recv()
            out[:, :, lanes(c)] = out[:, :, lanes(c)] + down_in[last - 1, :, :, lanes(c)]

    for step in range(grids - 1):
        for c in range(CHUNKS):
            @pl.when(z <= step)
            def _():
                up(step, c).wait_send()

            @pl.when(last - z <= step)
            def _():
                down(step, c).wait_send()


def high_low(values):
    high = values.astype(jnp.bfloat16)
    low = (values - high.astype(jnp.float32)).astype(jnp.bfloat16)
    return high, low


def exchange_kernel(
    batch, longest, pairs, weights, cutoff, own, visiting, planes, line, shells, screen,
    out_own, out_visiting, fields, outs, high, low, work,
):
    count, extent, cells = own.shape
    visitors = visiting.shape[0]
    half = cells // 2
    fields[:count] = own[...]
    fields[count:] = visiting[...]
    outs[...] = jnp.zeros_like(outs)

    def run_batch(step, _):
        def form(p, _):
            k = (step * batch + p) * 4
            a, b = pairs[k], pairs[k + 1]
            rows = pl.ds(pl.multiple_of(p * extent, extent), extent)
            near = fields[a, :, :half] * fields[b, :, :half]
            far = fields[a, :, half:] * fields[b, :, half:]
            for e, folded in enumerate((near + far, near - far)):
                high[e, rows, :], low[e, rows, :] = high_low(folded)
            return 0

        lax.fori_loop(0, batch, form, 0)

        def forward(e, _):
            total = jnp.dot(low[e], planes[e, 0], preferred_element_type=jnp.float32)
            total += jnp.dot(high[e], planes[e, 1], preferred_element_type=jnp.float32)
            total += jnp.dot(high[e], planes[e, 0], preferred_element_type=jnp.float32)
            work[e] = total
            return 0

        lax.fori_loop(0, 2, forward, 0)

        def screened(p, _):
            rows = pl.ds(pl.multiple_of(p * extent, extent), extent)
            for e in range(2):
                lanes = pl.ds(e * half, half)
                h, l = high_low(work[e, rows, :])
                spectrum = jnp.dot(
                    line[...], jnp.concatenate([h, l, h], axis=0),
                    preferred_element_type=jnp.float32,
                )
                factor = jnp.where(shells[:, lanes] <= cutoff[0], screen[:, lanes], 0.0)
                h, l = high_low(spectrum * factor)
                back = jnp.dot(
                    line[...], jnp.concatenate([h, l, h], axis=0),
                    preferred_element_type=jnp.float32,
                )
                high[e, rows, :], low[e, rows, :] = high_low(back)
            return 0

        lax.fori_loop(0, batch, screened, 0)

        def inverse(e, _):
            def product(left, right):
                return lax.dot_general(
                    left, right, (((1,), (1,)), ((), ())), preferred_element_type=jnp.float32
                )

            total = product(low[e], planes[e, 0])
            total += product(high[e], planes[e, 1])
            total += product(high[e], planes[e, 0])
            work[e] = total
            return 0

        lax.fori_loop(0, 2, inverse, 0)

        def apply(p, _):
            k = (step * batch + p) * 4
            a, b = pairs[k], pairs[k + 1]
            rows = pl.ds(pl.multiple_of(p * extent, extent), extent)
            to_a = -weights[b] * pairs[k + 2].astype(jnp.float32)
            to_b = -weights[a] * pairs[k + 3].astype(jnp.float32)
            even, odd = work[0, rows, :], work[1, rows, :]
            for lanes, v in ((pl.ds(0, half), even + odd), (pl.ds(half, half), even - odd)):
                phi_a, phi_b = fields[a, :, lanes], fields[b, :, lanes]
                outs[a, :, lanes] = outs[a, :, lanes] + to_a * (phi_b * v)
                outs[b, :, lanes] = outs[b, :, lanes] + to_b * (phi_a * v)
            return 0

        lax.fori_loop(0, batch, apply, 0)
        return 0

    lax.fori_loop(0, longest // batch, run_batch, 0)
    out_own[...] = outs[:count]
    out_visiting[...] = outs[count:]


def on_device(bands, grids, orbitals, occupation, cutoff):
    count, thickness, cells = orbitals.shape
    extent = thickness * grids
    planes, line, shells, screen = transform_tables(extent)
    table, longest, batch, parts = pair_lists(bands, grids, count)
    g = lax.axis_index("grid")
    band = lax.axis_index("band")
    weights = occupation.astype(jnp.float32) * 0.5
    visiting_weights = lax.ppermute(weights, ("band", "grid"), routes(bands, grids, parts))
    all_weights = jnp.concatenate([weights, visiting_weights])
    pairs = jnp.asarray(table)[g, band % 2]

    anywhere = pl.BlockSpec(memory_space=pl.ANY)
    dma = pltpu.SemaphoreType.DMA
    whole = jax.ShapeDtypeStruct((extent, count, cells), jnp.float32)
    gathered = pl.pallas_call(
        functools.partial(gather_kernel, bands, grids, parts),
        out_shape=(whole, whole),
        in_specs=[anywhere],
        out_specs=(anywhere, anywhere),
        scratch_shapes=[
            dma, dma((grids,)), dma((grids,)), dma((grids,)), dma((grids,)), dma((grids,)),
        ],
        compiler_params=pltpu.CompilerParams(collective_id=0, has_side_effects=True),
    )(orbitals.transpose(1, 0, 2))
    own, visiting = (x.transpose(1, 0, 2) for x in gathered)

    rows = batch * extent
    smem = pl.BlockSpec(memory_space=pltpu.SMEM)
    vmem = pl.BlockSpec(memory_space=pltpu.VMEM)
    slots = 2 * count
    out_own, out_visiting = pl.pallas_call(
        functools.partial(exchange_kernel, batch, longest),
        out_shape=(
            jax.ShapeDtypeStruct(own.shape, jnp.float32),
            jax.ShapeDtypeStruct(visiting.shape, jnp.float32),
        ),
        in_specs=[smem] * 3 + [vmem] * 6,
        out_specs=(vmem, vmem),
        scratch_shapes=[
            pltpu.VMEM((slots, extent, cells), jnp.float32),
            pltpu.VMEM((slots, extent, cells), jnp.float32),
            pltpu.VMEM((2, rows, cells // 2), jnp.bfloat16),
            pltpu.VMEM((2, rows, cells // 2), jnp.bfloat16),
            pltpu.VMEM((2, rows, cells // 2), jnp.float32),
        ],
        compiler_params=pltpu.CompilerParams(vmem_limit_bytes=56 * 1024 * 1024),
    )(
        pairs, all_weights, cutoff.reshape(1), own, visiting,
        jnp.asarray(planes), jnp.asarray(line), jnp.asarray(shells), jnp.asarray(screen),
    )
    steps = grids - 1
    slabs = pltpu.VMEM((steps, thickness, count, cells), jnp.float32)
    total = pl.pallas_call(
        functools.partial(reduce_kernel, bands, grids, parts),
        out_shape=jax.ShapeDtypeStruct((thickness, count, cells), jnp.float32),
        in_specs=[vmem, vmem],
        out_specs=vmem,
        scratch_shapes=[
            pltpu.VMEM((extent, count, cells), jnp.float32), slabs, slabs, slabs, slabs,
            *[dma((grids, CHUNKS))] * 2, *[dma((steps, CHUNKS))] * 4,
        ],
        compiler_params=pltpu.CompilerParams(
            collective_id=1, has_side_effects=True, vmem_limit_bytes=56 * 1024 * 1024
        ),
    )(out_own.transpose(1, 0, 2), out_visiting.transpose(1, 0, 2))
    return total.transpose(1, 0, 2)


def solution(mesh):
    placed = (P("band", "grid", None), P("band"), P())
    return jax.shard_map(
        functools.partial(on_device, mesh.shape["band"], mesh.shape["grid"]),
        mesh=mesh, in_specs=placed, out_specs=P("band", "grid", None), check_vma=False,
    )
```
